32 devices in a mesh: groups: 2 (over x), expert: 16 (over z, y, core).
Axes of the slice: x: 2, y: 2, z: 4, core: 2. Of those that a mesh axis runs over, the one named last changes fastest.
Arguments:
- hidden: bfloat16 [8192, 6, 1536], P(('groups', 'expert')), parts along dimension 0, may hold values from -6 to 6
- out_grad: bfloat16 [8192, 5120], P(('groups', 'expert')), parts along dimension 0, may hold values from -6 to 6
- gate_weights: float32 [8192, 6], P(('groups', 'expert')), parts along dimension 0, may hold values from 0.02 to 0.5
- expert_ids: int32 [8192, 6], P(('groups', 'expert')), parts along dimension 0, may hold values from 0 to 31, all different within a row; in each aligned block of 256 rows (0 to 255, 256 to 511, ...) at most 64 rows name the same one
- example_ids: int32 [8192], P(('groups', 'expert')), parts along dimension 0, may hold values from 0 to 31, as said below
- query_ids: int32 [64], P('groups'), parts along dimension 0, may hold values from 0 to 31
- in_factor: bfloat16 [32, 1536, 64], P('expert'), may hold values from -0.15625 to 0.15625
- out_factor: bfloat16 [5120, 64], replicated, may hold values from -0.078125 to 0.078125
Outputs:
- sketch: float32 [64, 4096], P(('groups', 'expert')), parts along dimension 0
- scores: float32 [64, 32], P(('groups', 'expert')), parts along dimension 0
The draws below stay inside these ranges and needn't reach their ends.
There are 2 independent parts, one for each index of `groups`. The reference program is written for one: setup_inputs(seed, part) draws one part's arguments, and reference() takes and returns one part's arrays. A program takes and returns all parts, laid end to end along the dimension named above; an argument that names none is the same for every part. Nothing has to cross between parts.
Inputs may be any that keep to these rules, and one draw needn't show every extreme that they name: `expert_ids`: each row names 6 different experts; in each aligned block of 256 rows no expert is named by more than 64 rows, a bound that some block reaches. `example_ids`: in aligned block b of 256 tokens the ids never fall and take every value from b * 2 to b * 2 + 1.
All inputs are finite; a program needn't handle non-finite values.
Results may differ from the reference program's by a relative error of at most 0.0003.
Values may be sent and summed in bfloat16 or wider, within the bound.
A program may use at most 128 MiB of HBM per device.

```python
import math
import jax
import jax.numpy as jnp
import numpy as np
from jax import lax

D = 5120
FF = 1536
TOP = 6
RANK = 64
TOK_DEV = 256
EX_DEV = 2
NQ = 32
EXPERTS = 32
CAP = 64
TOKENS = 4096
EXAMPLES = 32
N_EXPERT = 16


def draw_example_ids(key, part):
    key = jax.random.fold_in(key, 11)
    blocks = TOKENS // TOK_DEV
    subkeys = jax.random.split(key, blocks)
    shuffled = jax.vmap(lambda subkey: jax.random.permutation(subkey, TOK_DEV - 1))(subkeys)
    cut_points = shuffled[:, :EX_DEV - 1] + 1
    position = jnp.arange(TOK_DEV, dtype=jnp.int32)
    within = jnp.sum((position[None, :, None] >= cut_points[:, None, :]).astype(jnp.int32), axis=2)
    block_base = jnp.arange(blocks, dtype=jnp.int32)[:, None] * EX_DEV
    return (block_base + within).reshape(TOKENS).astype(jnp.int32)


def touch_ends(entries, rng, smallest, high):
    place = [jax.random.randint(jax.random.fold_in(rng, axis), (), 0, length) for axis, length in enumerate(entries.shape)]
    longest = entries.shape.index(max(entries.shape))
    neighbour = place[:longest] + [(place[longest] + 1) % entries.shape[longest]] + place[longest + 1:]
    return entries.at[tuple(place)].set(smallest).at[tuple(neighbour)].set(high)


def steps_of(key, extent, pieces, least, high):
    def one(dim, blocks):
        draws = jax.random.uniform(jax.random.fold_in(jax.random.fold_in(key, 6), dim), (blocks,), jnp.float32, least / len(pieces), high / len(pieces))
        return jnp.repeat(jnp.exp(draws), extent[dim] // blocks).reshape((-1,) + (1,) * (len(extent) - dim - 1))

    loudness = one(*pieces[0])
    for cut in pieces[1:]:
        loudness = loudness * one(*cut)
    return loudness


def routed_block(own_key, own, number, rows, number_of, top, limit, skew):
    ranking = jax.random.permutation(own_key, number_of)
    heavy_load, common = load_shares(number_of, rows * top, limit, skew, True), load_shares(number_of, rows * top, limit, skew, False)
    places = jnp.arange(number_of)

    def named(lengths, turn):
        used = int((lengths > 0).sum())
        fixed = max(1, used // 4)
        passed = fixed + (places - fixed + turn * (used - fixed)) % max(1, number_of - fixed)
        return jnp.zeros((number_of,), jnp.int32).at[ranking[jnp.where(places < fixed, places, passed)]].set(jnp.asarray(lengths, jnp.int32))

    lengths = jnp.where(number % 4 == 0, named(heavy_load, number // 4), named(common, number - number // 4 - 1))
    mixed = jax.random.permutation(jax.random.fold_in(own, 3), number_of)
    donor, receiver = mixed[0:number_of // 2 * 2:2], mixed[1:number_of // 2 * 2:2]
    margin = jnp.minimum(lengths[donor] - 1, limit - lengths[receiver]) // 2
    margin = jnp.where((donor == ranking[0]) | (receiver == ranking[0]) | (lengths[receiver] == 0), 0, jnp.maximum(margin, 0))
    passed = jax.random.randint(jax.random.fold_in(own, 4), (number_of // 2,), 0, 1 << 20) % (margin + 1)
    lengths = lengths.at[donor].add(-passed).at[receiver].add(passed)
    labels = jnp.searchsorted(jnp.cumsum(lengths), jnp.arange(rows * top), side="right").astype(jnp.int32)
    listing = labels.reshape(top, rows).T
    listing = listing[jax.random.permutation(jax.random.fold_in(own, 1), rows)]
    turn = jax.random.randint(jax.random.fold_in(own, 2), (rows, 1), 0, top)
    return jnp.take_along_axis(listing, (jnp.arange(top)[None, :] + turn) % top, axis=1)


def load_shares(amount, total, most, lean, full):
    weights = [(1 << 20) // math.isqrt(grade ** lean) + 1 for grade in range(1, amount + 1)]
    largest = most if full else min(most, max(-(-total // amount), total * weights[0] // sum(weights)))
    least = 1 if total - largest >= amount - 1 else 0
    counts, surplus = [largest] + [least] * (amount - 1), total - largest - least * (amount - 1)
    while surplus > 0:
        candidates = [i for i in range(1, amount) if counts[i] < largest] or [i for i in range(1, amount) if counts[i] < most]
        mass, budget = sum([weights[i] for i in candidates]), surplus
        for i in candidates:
            addition = min(most - counts[i], max(1, budget * weights[i] // mass), surplus)
            counts[i] = counts[i] + addition
            surplus = surplus - addition
    return np.array(counts)


def gaussian(key, shape, width, most, cuts=(), kind=jnp.bfloat16):
    array = width * jax.random.normal(key, shape, jnp.float32)
    if cuts:
        array = array * steps_of(key, shape, cuts, -0.22, 0.18)
    return jnp.clip(array, -most, most).astype(kind)


def setup_inputs(seed: int = 0, part: int = 0) -> dict:
    keys = jax.random.split(jax.random.key(seed), 9)
    part_keys = jax.random.split(jax.random.fold_in(keys[8], part), 9)
    hidden = gaussian(part_keys[0], (TOKENS, TOP, FF), 1.0, 6.0, ((0, 16),))
    out_grad = gaussian(part_keys[1], (TOKENS, D), 1.0, 6.0, ((0, 16),))
    gate_weights = jnp.clip(jnp.exp(math.log(0.5) - 3.218876 * jax.random.uniform(part_keys[2], (TOKENS, TOP), jnp.float32) ** steps_of(part_keys[2], (TOKENS, TOP), ((0, 16),), -0.2, 0.2)), 0.02, 0.5)
    expert_ids_keys = jax.random.split(jax.random.fold_in(part_keys[3], 1), TOKENS // TOK_DEV)
    expert_ids_turns = jax.random.permutation(jax.random.fold_in(part_keys[3], 3), TOKENS // TOK_DEV)
    expert_ids = jax.vmap(lambda own, number: routed_block(jax.random.fold_in(part_keys[3], 2), own, number, TOK_DEV, EXPERTS, TOP, CAP, 2))(expert_ids_keys, expert_ids_turns).reshape((TOKENS, TOP))
    example_ids = draw_example_ids(jax.random.fold_in(jax.random.fold_in(keys[8], part), 71), part)
    query_ids = touch_ends(jax.random.randint(part_keys[5], (NQ,), 0, EXAMPLES), jax.random.fold_in(part_keys[5], 1), 0, EXAMPLES - 1).astype(jnp.int32)
    in_factor = gaussian(keys[6], (EXPERTS, FF, RANK), FF ** -0.5, 0.15625, ((0, 16),))
    out_factor = gaussian(keys[7], (D, RANK), D ** -0.5, 0.078125)
    return dict(hidden=hidden, out_grad=out_grad, gate_weights=gate_weights, expert_ids=expert_ids, example_ids=example_ids, query_ids=query_ids, in_factor=in_factor, out_factor=out_factor)


sketch_scale = 0.125
score_scale = 1.0 / 512.0
epsilon = 1e-06

def reference(hidden, out_grad, gate_weights, expert_ids, example_ids, query_ids, in_factor, out_factor):
    slot_total = TOKENS * TOP
    max_rows = N_EXPERT * CAP
    slot_expert = expert_ids.reshape(slot_total).astype(jnp.int32)
    slot_order = jnp.argsort(slot_expert, stable=True).astype(jnp.int32)
    sorted_ids = slot_expert[slot_order]
    starts = jnp.searchsorted(sorted_ids, jnp.arange(EXPERTS, dtype=jnp.int32), side='left').astype(jnp.int32)
    rank_sorted = jnp.arange(slot_total, dtype=jnp.int32) - starts[sorted_ids]
    slot_rank = jnp.zeros((slot_total,), jnp.int32).at[slot_order].set(rank_sorted)
    slot_place = slot_expert * max_rows + slot_rank
    buffer = jnp.zeros((EXPERTS * max_rows, FF), jnp.bfloat16)
    buffer = buffer.at[slot_place].set(hidden.reshape(slot_total, FF)).reshape(EXPERTS, max_rows, FF)

    def project_expert(inputs):
        return jnp.dot(inputs[0], inputs[1], preferred_element_type=jnp.float32)
    projected = lax.map(project_expert, (buffer, in_factor))
    slot_proj = projected.reshape(EXPERTS * max_rows, RANK)[slot_place]
    grad_proj = jnp.dot(out_grad, out_factor, preferred_element_type=jnp.float32)
    grad_slot = jnp.repeat(grad_proj, TOP, axis=0)
    example_local = jnp.repeat(example_ids % EX_DEV, TOP)
    weight_slot = (example_local[:, None] == jnp.arange(EX_DEV, dtype=jnp.int32)[None, :]).astype(jnp.float32)
    weight_slot = weight_slot * gate_weights.reshape(slot_total, 1).astype(jnp.float32)

    def block_sketch(inputs):
        weights, proj, grads = inputs
        return jnp.einsum('rx,ri,rj->xij', weights, proj, grads, precision=lax.Precision.HIGHEST).reshape(EX_DEV, RANK * RANK)
    block_rows = TOK_DEV * TOP
    sums = lax.map(block_sketch, (weight_slot.reshape(N_EXPERT, block_rows, EX_DEV), slot_proj.reshape(N_EXPERT, block_rows, RANK), grad_slot.reshape(N_EXPERT, block_rows, RANK)))
    sketch = sums.reshape(EXAMPLES, RANK * RANK) * sketch_scale
    queries = sketch[query_ids.astype(jnp.int32)]
    row_scale = lax.rsqrt(lax.optimization_barrier(jnp.mean(sketch * sketch, axis=1)) + epsilon)
    query_scale = lax.rsqrt(lax.optimization_barrier(jnp.mean(queries * queries, axis=1)) + epsilon)
    scores = jnp.dot(sketch, queries.T, precision=lax.Precision.HIGHEST)
    scores = scores * row_scale[:, None] * query_scale[None, :] * score_scale
    return (sketch, scores)
```

```python
import functools

import jax
import jax.numpy as jnp
from jax import lax
from jax.experimental import pallas as pl
from jax.experimental.pallas import tpu as pltpu
from jax.sharding import PartitionSpec as P

EX_DEV = 2
PARTS = 3

sketch_scale = 0.125
score_scale = 1.0 / 512.0
epsilon = 1e-06

MESH = pl.DeviceIdType.MESH
HIGHEST = lax.Precision.HIGHEST
NT = (((1,), (1,)), ((), ()))


def kernel(
    n, hid_hbm, og_hbm, of_hbm, w_hbm, info_ref, qcol_ref,
    sketch_ref, scores_ref,
    wall, x_ref, og_ref, of_ref, ids_ref, gate_ref, acc_ref, gm_ref,
    part_out, part_in, gram_out, gram_in,
    send_sem, recv_sem, local_sem, s1_send, s1_recv, s2_send, s2_recv,
):
    g = lax.axis_index("groups")
    e = lax.axis_index("expert")
    zn = n // 4
    core = e % 2
    y = (e // 2) % 2
    z = e // 4
    tokens = gm_ref.shape[0]
    top = x_ref.shape[0] // tokens
    width = wall.shape[3]
    half = part_out.shape[0]

    own_loads = [
        pltpu.make_async_copy(
            w_hbm.at[:, p * width : (p + 1) * width], wall.at[e, p], local_sem.at[p]
        )
        for p in range(PARTS)
    ]
    og_load = pltpu.make_async_copy(og_hbm, og_ref, local_sem.at[3])
    of_load = pltpu.make_async_copy(of_hbm, of_ref, local_sem.at[4])
    x_load = pltpu.make_async_copy(hid_hbm, x_ref, local_sem.at[5])
    for load in own_loads + [og_load, of_load, x_load]:
        load.start()

    barrier = pltpu.get_barrier_semaphore()
    g_other = g + 1 - 2 * (g % 2)

    def greet(off, carry):
        pl.semaphore_signal(
            barrier, inc=1, device_id=(g, lax.rem(e + off, n)), device_id_type=MESH
        )
        return carry

    lax.fori_loop(1, n, greet, 0)
    pl.semaphore_signal(barrier, inc=1, device_id=(g_other, e), device_id_type=MESH)
    pl.semaphore_wait(barrier, n)

    mine = 2 * (g % 2)
    theirs = 2 - mine

    def shard(col, zz, cc):
        return (zz * 2 + col) * 2 + cc

    up = (g, shard(y, jnp.minimum(z + 1, zn - 1), core))
    down = (g, shard(y, jnp.maximum(z - 1, 0), core))
    across = (g, shard(1 - y, z, core))
    other_x = (g_other, e)
    sibling = (g, shard(y, z, 1 - core))
    targets = (up, down, across, other_x, sibling)
    UP, DOWN, ACROSS, OTHER_X, SIBLING = range(5)

    def copy(kind, s, p):
        return pltpu.make_async_remote_copy(
            src_ref=wall.at[s, p],
            dst_ref=wall.at[s, p],
            send_sem=send_sem.at[kind, s // 2, p],
            recv_sem=recv_sem.at[s, p],
            device_id=targets[kind],
            device_id_type=MESH,
        )

    def arrived(s, p):
        copy(SIBLING, s, p).wait_recv()

    for load in own_loads:
        load.wait()

    def own_sends(act):
        for p in (mine, 1):
            act(ACROSS, e, p)
            pl.when(z + 1 < zn)(lambda p=p: act(UP, e, p))
            pl.when(z >= 1)(lambda p=p: act(DOWN, e, p))
        for p in range(PARTS):
            act(SIBLING, e, p)

    def start(kind, s, p):
        copy(kind, s, p).start()

    def finish(kind, s, p):
        copy(kind, s, p).wait_send()

    own_sends(start)

    table = jnp.transpose(info_ref[...])
    lane = lax.broadcasted_iota(jnp.int32, (tokens, 128), 1)
    upper = lane >= 64
    upper_f = upper.astype(jnp.float32)
    for k in range(top):
        rows = pl.ds(k * tokens, tokens)
        ids_ref[rows, :] = jnp.broadcast_to(table[:, k : k + 1], (tokens, 128)) - upper_f
        gate_ref[rows, :] = jnp.broadcast_to(table[:, top + k : top + k + 1], (tokens, 128))
    example = jnp.broadcast_to(table[:, 2 * top : 2 * top + 1], (tokens, 128))
    acc_ref[...] = jnp.zeros_like(acc_ref)
    gram_out[...] = jnp.zeros_like(gram_out)
    og_load.wait()
    of_load.wait()
    factor = of_ref[...]
    proj = lax.dot_general(
        og_ref[...], jnp.concatenate([factor, factor], axis=0), NT,
        preferred_element_type=jnp.float32,
    )
    gm_ref[...] = jnp.where(example == upper_f, proj * sketch_scale, 0.0)
    x_load.wait()

    def from_z(r, act):
        for kind, zs, onward in ((UP, z - r, z + 1 < zn), (DOWN, z + r, z >= 1)):

            @pl.when((zs >= 0) & (zs < zn))
            def _(kind=kind, zs=zs, onward=onward):
                s = shard(y, zs, core)
                for p in (mine, 1):
                    if act is start:
                        arrived(s, p)
                    pl.when(onward)(lambda p=p: act(kind, s, p))
                    act(ACROSS, s, p)
                    if p is mine:
                        act(OTHER_X, s, p)
                    act(SIBLING, s, p)

    def from_y(r, act):
        def one(i, carry):
            zs = z + r * (2 * i - 1)

            @pl.when((zs >= 0) & (zs < zn) & ((r > 0) | (i == 0)))
            def _():
                s = shard(1 - y, zs, core)
                for p in (mine, 1):
                    if act is start:
                        arrived(s, p)
                    if p is mine:
                        act(OTHER_X, s, p)
                    act(SIBLING, s, p)

            return carry

        lax.fori_loop(0, 2, one, 0)

    def from_x(r, act):
        def one(i, carry):
            zs = z + r * (2 * (i // 2) - 1)
            col = i % 2

            @pl.when((zs >= 0) & (zs < zn) & ((r > 0) | ((i // 2 == 0) & (col != y))))
            def _():
                s = shard(col, zs, core)
                if act is start:
                    arrived(s, theirs)
                act(SIBLING, s, theirs)

            return carry

        lax.fori_loop(0, 4, one, 0)

    def compute(r):
        def one(i, carry):
            zs = z + r * (2 * (i // 2) - 1)
            col = i % 2

            @pl.when((zs >= 0) & (zs < zn) & ((r > 0) | (i // 2 == 0)))
            def _():
                place = zs * 2 + col
                for p in range(PARTS):
                    arrived(place * 2 + 1 - core, p)
                weights = jnp.concatenate(
                    [
                        jnp.concatenate([wall[2 * place + h, p] for p in range(PARTS)], axis=1)
                        for h in range(2)
                    ],
                    axis=0,
                )
                prod = lax.dot_general(
                    x_ref[...], weights, NT, preferred_element_type=jnp.float32
                )
                first = (4 * place).astype(jnp.float32)
                total = acc_ref[...]
                for k in range(top):
                    rows = slice(k * tokens, (k + 1) * tokens)
                    ids = ids_ref[rows, :]
                    chosen = jnp.where(
                        ids == first,
                        prod[rows, :128],
                        jnp.where(ids == first + 2.0, prod[rows, 128:], 0.0),
                    )
                    total = total + gate_ref[rows, :] * chosen
                acc_ref[...] = total

            return carry

        lax.fori_loop(0, 4, one, 0)

    def step(t, carry):
        pl.when(t + 1 < zn)(lambda: from_z(t + 1, start))
        pl.when(t < zn)(lambda: from_y(t, start))
        pl.when(t >= 1)(lambda: compute(t - 1))
        pl.when(t < zn)(lambda: from_x(t, start))
        return carry

    lax.fori_loop(0, zn + 1, step, 0)

    pre = lax.dot_general(
        jnp.transpose(acc_ref[...]), gm_ref[...], (((1,), (0,)), ((), ())),
        precision=HIGHEST, preferred_element_type=jnp.float32,
    )
    sk = pre[:64] + pre[64:]
    sketch_ref[...] = sk
    rows_each = part_out.shape[1]
    for d in range(n):
        part_out[d] = sk[d * rows_each : (d + 1) * rows_each]

    def exchange(src, dst, send, recv, off):
        to = lax.rem(e + off, n)
        return pltpu.make_async_remote_copy(
            src_ref=src.at[to], dst_ref=dst.at[e],
            send_sem=send.at[to], recv_sem=recv.at[e],
            device_id=(g, to), device_id_type=MESH,
        )

    def incoming(src, dst, send, recv, off):
        frm = lax.rem(e + off, n)
        return pltpu.make_async_remote_copy(
            src_ref=src.at[frm], dst_ref=dst.at[frm],
            send_sem=send.at[frm], recv_sem=recv.at[frm],
            device_id=(g, frm), device_id_type=MESH,
        )

    def every(act):
        def one(off, carry):
            act(off)
            return carry

        lax.fori_loop(1, n, one, 0)

    one_set = (part_out, part_in, s1_send, s1_recv)
    two_set = (gram_out, gram_in, s2_send, s2_recv)
    every(lambda off: exchange(*one_set, off).start())
    part_in[e] = part_out[e]
    every(lambda off: incoming(*one_set, off).wait_recv())

    slabs = [part_in[:, i, :] for i in range(rows_each)]
    zmat = jnp.concatenate(
        [
            jnp.concatenate([slab[:, :64] for slab in slabs], axis=1),
            jnp.concatenate([slab[:, 64:] for slab in slabs], axis=1),
        ],
        axis=0,
    )
    gram = lax.dot_general(
        zmat, zmat, NT, precision=HIGHEST, preferred_element_type=jnp.float32
    )
    pairs = 2 * half
    eye = lax.broadcasted_iota(jnp.int32, (pairs, pairs), 0) == lax.broadcasted_iota(
        jnp.int32, (pairs, pairs), 1
    )
    diag = jnp.sum(jnp.where(eye, gram, 0.0), axis=0, keepdims=True)
    gram_out[:, 0, :pairs] = gram[:half]
    gram_out[:, 1, :pairs] = gram[half:]
    gram_out[:, 2, :pairs] = jnp.broadcast_to(diag, (half, pairs))
    every(lambda off: exchange(*two_set, off).start())
    gram_in[e] = gram_out[e]
    every(lambda off: incoming(*two_set, off).wait_recv())
    total = jnp.sum(gram_in[...], axis=0)

    count = qcol_ref.shape[1]
    pick = (
        lax.broadcasted_iota(jnp.int32, (128, count), 0)
        == jnp.broadcast_to(qcol_ref[...], (128, count))
    ).astype(jnp.float32)
    raw = jnp.dot(total, pick, precision=HIGHEST, preferred_element_type=jnp.float32)
    size = sk.shape[0] * 64
    query_scale = lax.rsqrt(raw[2:3] * (1.0 / size) + epsilon)
    place = lax.broadcasted_iota(jnp.int32, (2, 128), 0) * n + e
    own = lax.broadcasted_iota(jnp.int32, (2, 128), 1) == place
    norm = jnp.sum(jnp.where(own, total[0:2], 0.0), axis=1, keepdims=True)
    row_scale = lax.rsqrt(norm * (1.0 / size) + epsilon)
    scores_ref[...] = raw[0:2] * row_scale * query_scale * score_scale

    own_sends(finish)

    def drain(r, carry):
        pl.when(r >= 1)(lambda: from_z(r, finish))
        from_y(r, finish)
        from_x(r, finish)
        return carry

    lax.fori_loop(0, zn, drain, 0)
    every(lambda off: exchange(*one_set, off).wait_send())
    every(lambda off: exchange(*two_set, off).wait_send())


def on_device(
    hidden, out_grad, gate_weights, expert_ids, example_ids, query_ids, in_factor, out_factor
):
    n = lax.axis_size("expert")
    tokens, top, feat = hidden.shape
    exp_local = in_factor.shape[0]
    rank = out_factor.shape[1]
    model = out_grad.shape[1]
    queries = query_ids.shape[0]
    hid = jnp.transpose(hidden, (1, 0, 2)).reshape(top * tokens, feat)
    w = jnp.transpose(in_factor, (0, 2, 1)).reshape(exp_local * rank, feat)
    factor = out_factor.T
    info = jnp.concatenate(
        [
            expert_ids.T.astype(jnp.float32),
            gate_weights.T,
            (example_ids % EX_DEV).astype(jnp.float32)[None, :],
            jnp.zeros((16 - 2 * top - 1, tokens), jnp.float32),
        ],
        axis=0,
    )
    qcol = ((query_ids % EX_DEV) * n + query_ids // EX_DEV)[None, :]
    any_spec = pl.BlockSpec(memory_space=pl.ANY)
    vmem = pl.BlockSpec(memory_space=pltpu.VMEM)
    rows_each = rank // n
    f32, bf16 = jnp.float32, jnp.bfloat16
    sketch, scores = pl.pallas_call(
        functools.partial(kernel, n),
        out_shape=(
            jax.ShapeDtypeStruct((rank, EX_DEV * rank), f32),
            jax.ShapeDtypeStruct((EX_DEV, queries), f32),
        ),
        in_specs=[any_spec] * 4 + [vmem] * 2,
        out_specs=(vmem, vmem),
        scratch_shapes=[
            pltpu.VMEM((n, PARTS, exp_local * rank, feat // PARTS), bf16),
            pltpu.VMEM((top * tokens, feat), bf16),
            pltpu.VMEM((tokens, model), bf16),
            pltpu.VMEM((rank, model), bf16),
            pltpu.VMEM((top * tokens, 128), f32),
            pltpu.VMEM((top * tokens, 128), f32),
            pltpu.VMEM((tokens, 128), f32),
            pltpu.VMEM((tokens, 128), f32),
            pltpu.VMEM((n, rows_each, 128), f32),
            pltpu.VMEM((n, rows_each, 128), f32),
            pltpu.VMEM((n, 8, 128), f32),
            pltpu.VMEM((n, 8, 128), f32),
            pltpu.SemaphoreType.DMA((5, n // 2, PARTS)),
            pltpu.SemaphoreType.DMA((n, PARTS)),
            pltpu.SemaphoreType.DMA((6,)),
            pltpu.SemaphoreType.DMA((n,)),
            pltpu.SemaphoreType.DMA((n,)),
            pltpu.SemaphoreType.DMA((n,)),
            pltpu.SemaphoreType.DMA((n,)),
        ],
        compiler_params=pltpu.CompilerParams(
            collective_id=0, has_side_effects=True, vmem_limit_bytes=52 * 1024 * 1024
        ),
    )(hid, out_grad, factor, w, info, qcol)
    sketch = jnp.transpose(sketch.reshape(rank, EX_DEV, rank), (1, 0, 2))
    return (sketch.reshape(EX_DEV, rank * rank), scores)


def solution(mesh):
    in_specs = (
        P(("groups", "expert"), None, None),
        P(("groups", "expert"), None),
        P(("groups", "expert"), None),
        P(("groups", "expert"), None),
        P(("groups", "expert")),
        P("groups"),
        P("expert", None, None),
        P(),
    )
    out_specs = (P(("groups", "expert"), None), P(("groups", "expert"), None))
    return jax.shard_map(
        on_device, mesh=mesh, in_specs=in_specs, out_specs=out_specs, check_vma=False
    )
```

```python
import functools

import jax
import jax.numpy as jnp
from jax import lax
from jax.experimental import pallas as pl
from jax.experimental.pallas import tpu as pltpu
from jax.sharding import PartitionSpec as P

EX_DEV = 2
PARTS = 3

sketch_scale = 0.125
score_scale = 1.0 / 512.0
epsilon = 1e-06

MESH = pl.DeviceIdType.MESH
HIGHEST = lax.Precision.HIGHEST
NT = (((1,), (1,)), ((), ()))


def kernel(
    n, hid_hbm, og_hbm, of_hbm, w_hbm, ids_hbm, gates_hbm, example_hbm, query_hbm,
    sketch_ref, scores_ref,
    ids_in, gates_in, example_in, query_in, info_ref, sk_ref,
    wall, x_ref, og_ref, of_ref, ids_ref, gate_ref, acc_ref, gm_ref,
    part_out, part_in, gram_out, gram_in,
    send_sem, recv_sem, local_sem, s1_send, s1_recv, s2_send, s2_recv,
):
    g = lax.axis_index("groups")
    e = lax.axis_index("expert")
    zn = n // 4
    core = e % 2
    y = (e // 2) % 2
    z = e // 4
    tokens = gm_ref.shape[0]
    top = x_ref.shape[0] // tokens
    width = wall.shape[3]
    half = part_out.shape[0]

    barrier = pltpu.get_barrier_semaphore()
    g_other = g + 1 - 2 * (g % 2)
    pl.semaphore_signal(barrier, inc=1, device_id=(g_other, e), device_id_type=MESH)

    def greet(off, carry):
        pl.semaphore_signal(
            barrier, inc=1, device_id=(g, lax.rem(e + off, n)), device_id_type=MESH
        )
        return carry

    lax.fori_loop(1, n, greet, 0)

    own_loads = [
        pltpu.make_async_copy(
            w_hbm.at[:, p * width : (p + 1) * width], wall.at[e, p], local_sem.at[p]
        )
        for p in range(PARTS)
    ]
    og_load = pltpu.make_async_copy(og_hbm, og_ref, local_sem.at[3])
    of_load = pltpu.make_async_copy(of_hbm, of_ref, local_sem.at[4])
    x_load = pltpu.make_async_copy(hid_hbm, x_ref, local_sem.at[5])
    small_loads = [
        pltpu.make_async_copy(src, dst, local_sem.at[6 + i])
        for i, (src, dst) in enumerate(
            (
                (ids_hbm, ids_in),
                (gates_hbm, gates_in),
                (example_hbm, example_in),
                (query_hbm, query_in),
            )
        )
    ]
    for load in own_loads + small_loads + [og_load, of_load, x_load]:
        load.start()
    info_ref[...] = jnp.zeros_like(info_ref)
    acc_ref[...] = jnp.zeros_like(acc_ref)
    gram_out[...] = jnp.zeros_like(gram_out)

    pl.semaphore_wait(barrier, n)

    mine = 2 * (g % 2)
    theirs = 2 - mine

    def shard(col, zz, cc):
        return (zz * 2 + col) * 2 + cc

    up = (g, shard(y, jnp.minimum(z + 1, zn - 1), core))
    down = (g, shard(y, jnp.maximum(z - 1, 0), core))
    across = (g, shard(1 - y, z, core))
    other_x = (g_other, e)
    sibling = (g, shard(y, z, 1 - core))
    targets = (up, down, across, other_x, sibling)
    UP, DOWN, ACROSS, OTHER_X, SIBLING = range(5)

    def copy(kind, s, p):
        return pltpu.make_async_remote_copy(
            src_ref=wall.at[s, p],
            dst_ref=wall.at[s, p],
            send_sem=send_sem.at[kind, s // 2, p],
            recv_sem=recv_sem.at[s, p],
            device_id=targets[kind],
            device_id_type=MESH,
        )

    def arrived(s, p):
        copy(SIBLING, s, p).wait_recv()

    for load in own_loads:
        load.wait()

    def own_sends(act):
        for p in (mine, 1):
            act(ACROSS, e, p)
            pl.when(z + 1 < zn)(lambda p=p: act(UP, e, p))
            pl.when(z >= 1)(lambda p=p: act(DOWN, e, p))
        for p in range(PARTS):
            act(SIBLING, e, p)

    def start(kind, s, p):
        copy(kind, s, p).start()

    def finish(kind, s, p):
        copy(kind, s, p).wait_send()

    own_sends(start)

    for load in small_loads:
        load.wait()
    info_ref[0:top, :] = ids_in[...].astype(jnp.float32)
    info_ref[top : 2 * top, :] = gates_in[...]
    info_ref[2 * top : 2 * top + 1, :] = lax.rem(example_in[...], EX_DEV).astype(jnp.float32)
    table = jnp.transpose(info_ref[...])
    lane = lax.broadcasted_iota(jnp.int32, (tokens, 128), 1)
    upper = lane >= 64
    upper_f = upper.astype(jnp.float32)
    for k in range(top):
        rows = pl.ds(k * tokens, tokens)
        ids_ref[rows, :] = jnp.broadcast_to(table[:, k : k + 1], (tokens, 128)) - upper_f
        gate_ref[rows, :] = jnp.broadcast_to(table[:, top + k : top + k + 1], (tokens, 128))
    example = jnp.broadcast_to(table[:, 2 * top : 2 * top + 1], (tokens, 128))
    og_load.wait()
    of_load.wait()
    factor = of_ref[...]
    proj = lax.dot_general(
        og_ref[...], jnp.concatenate([factor, factor], axis=0), NT,
        preferred_element_type=jnp.float32,
    )
    gm_ref[...] = jnp.where(example == upper_f, proj * sketch_scale, 0.0)
    x_load.wait()

    def from_z(r, p, act):
        for kind, zs, onward in ((UP, z - r, z + 1 < zn), (DOWN, z + r, z >= 1)):

            @pl.when((zs >= 0) & (zs < zn))
            def _(kind=kind, zs=zs, onward=onward):
                s = shard(y, zs, core)
                if act is start:
                    arrived(s, p)
                pl.when(onward)(lambda: act(kind, s, p))
                act(ACROSS, s, p)
                if p is mine:
                    act(OTHER_X, s, p)
                act(SIBLING, s, p)

    def at_distance(r, body):
        def one(i, carry):
            zs = z + r * (2 * i - 1)
            pl.when((zs >= 0) & (zs < zn) & ((r > 0) | (i == 0)))(lambda: body(zs))
            return carry

        lax.fori_loop(0, 2, one, 0)

    def from_y(r, p, act):
        def body(zs):
            s = shard(1 - y, zs, core)
            if act is start:
                arrived(s, p)
            if p is mine:
                act(OTHER_X, s, p)
            act(SIBLING, s, p)

        at_distance(r, body)

    def from_x(r, col, act):
        def body(zs):
            s = shard(col, zs, core)
            if act is start:
                arrived(s, theirs)
            act(SIBLING, s, theirs)

        at_distance(r, body)

    def compute(r, col):
        def body(zs):
            place = zs * 2 + col
            for p in range(PARTS):
                arrived(place * 2 + 1 - core, p)
            weights = jnp.concatenate(
                [
                    jnp.concatenate([wall[2 * place + h, p] for p in range(PARTS)], axis=1)
                    for h in range(2)
                ],
                axis=0,
            )
            prod = lax.dot_general(
                x_ref[...], weights, NT, preferred_element_type=jnp.float32
            )
            first = (4 * place).astype(jnp.float32)
            total = acc_ref[...]
            for k in range(top):
                rows = slice(k * tokens, (k + 1) * tokens)
                ids = ids_ref[rows, :]
                chosen = jnp.where(
                    ids == first,
                    prod[rows, :128],
                    jnp.where(ids == first + 2.0, prod[rows, 128:], 0.0),
                )
                total = total + gate_ref[rows, :] * chosen
            acc_ref[...] = total

        at_distance(r, body)

    def step(t, carry):
        further = t + 1 < zn
        inside = t < zn

        @pl.when(further)
        def _():
            from_z(t + 1, mine, start)

        @pl.when(inside)
        def _():
            from_y(t, mine, start)

        @pl.when(t >= 1)
        def _():
            from_x(t - 1, 1 - y, start)

        def product(half_step, carry):
            col = jnp.where(half_step == 0, y, 1 - y)
            r = t - half_step

            @pl.when((r >= 0) & (r < zn))
            def _():
                compute(r, col)

            @pl.when((half_step == 0) & further)
            def _():
                from_z(t + 1, 1, start)

            @pl.when((half_step == 0) & inside)
            def _():
                from_y(t, 1, start)

            @pl.when((half_step == 0) & further)
            def _():
                from_x(t + 1, y, start)

            return carry

        lax.fori_loop(0, 2, product, 0)
        return carry

    lax.fori_loop(0, zn + 1, step, 0)

    pre = lax.dot_general(
        jnp.transpose(acc_ref[...]), gm_ref[...], (((1,), (0,)), ((), ())),
        precision=HIGHEST, preferred_element_type=jnp.float32,
    )
    sk = pre[:64] + pre[64:]
    rows_each = part_out.shape[1]
    for d in range(n):
        part_out[d] = sk[d * rows_each : (d + 1) * rows_each]

    def exchange(src, dst, send, recv, off):
        to = lax.rem(e + off, n)
        return pltpu.make_async_remote_copy(
            src_ref=src.at[to], dst_ref=dst.at[e],
            send_sem=send.at[to], recv_sem=recv.at[e],
            device_id=(g, to), device_id_type=MESH,
        )

    def incoming(src, dst, send, recv, off):
        frm = lax.rem(e + off, n)
        return pltpu.make_async_remote_copy(
            src_ref=src.at[frm], dst_ref=dst.at[frm],
            send_sem=send.at[frm], recv_sem=recv.at[frm],
            device_id=(g, frm), device_id_type=MESH,
        )

    def every(act):
        def one(off, carry):
            act(off)
            return carry

        lax.fori_loop(1, n, one, 0)

    one_set = (part_out, part_in, s1_send, s1_recv)
    two_set = (gram_out, gram_in, s2_send, s2_recv)
    every(lambda off: exchange(*one_set, off).start())
    part_in[e] = part_out[e]

    sk_ref[...] = sk
    even = sk_ref[pl.ds(0, sk.shape[0] // 2, stride=2), :]
    odd = sk_ref[pl.ds(1, sk.shape[0] // 2, stride=2), :]
    low = lax.broadcasted_iota(jnp.int32, even.shape, 1) < 64
    sketch_ref[:, 0, :] = jnp.where(low, even, pltpu.roll(odd, 64, 1))
    sketch_ref[:, 1, :] = jnp.where(low, pltpu.roll(even, 64, 1), odd)
    own_sends(finish)

    def drain(r, carry):
        for p in (mine, 1):
            pl.when(r >= 1)(lambda p=p: from_z(r, p, finish))
            from_y(r, p, finish)
        from_x(r, 1 - y, finish)
        pl.when(r >= 1)(lambda: from_x(r, y, finish))
        return carry

    lax.fori_loop(0, zn, drain, 0)
    every(lambda off: incoming(*one_set, off).wait_recv())

    slabs = [part_in[:, i, :] for i in range(rows_each)]
    zmat = jnp.concatenate(
        [
            jnp.concatenate([slab[:, :64] for slab in slabs], axis=1),
            jnp.concatenate([slab[:, 64:] for slab in slabs], axis=1),
        ],
        axis=0,
    )
    gram = lax.dot_general(
        zmat, zmat, NT, precision=HIGHEST, preferred_element_type=jnp.float32
    )
    pairs = 2 * half
    eye = lax.broadcasted_iota(jnp.int32, (pairs, pairs), 0) == lax.broadcasted_iota(
        jnp.int32, (pairs, pairs), 1
    )
    diag = jnp.sum(jnp.where(eye, gram, 0.0), axis=0, keepdims=True)
    gram_out[:, 0, :pairs] = gram[:half]
    gram_out[:, 1, :pairs] = gram[half:]
    gram_out[:, 2, :pairs] = jnp.broadcast_to(diag, (half, pairs))
    every(lambda off: exchange(*two_set, off).start())
    gram_in[e] = gram_out[e]
    every(lambda off: exchange(*one_set, off).wait_send())
    every(lambda off: incoming(*two_set, off).wait_recv())
    total = jnp.sum(gram_in[...], axis=0)

    query = query_in[...]
    column = lax.rem(query, EX_DEV) * n + lax.div(query, EX_DEV)
    count = query.shape[1]
    pick = (
        lax.broadcasted_iota(jnp.int32, (128, count), 0)
        == jnp.broadcast_to(column, (128, count))
    ).astype(jnp.float32)
    raw = jnp.dot(total, pick, precision=HIGHEST, preferred_element_type=jnp.float32)
    size = sk.shape[0] * 64
    query_scale = lax.rsqrt(raw[2:3] * (1.0 / size) + epsilon)
    place = lax.broadcasted_iota(jnp.int32, (2, 128), 0) * n + e
    own = lax.broadcasted_iota(jnp.int32, (2, 128), 1) == place
    norm = jnp.sum(jnp.where(own, total[0:2], 0.0), axis=1, keepdims=True)
    row_scale = lax.rsqrt(norm * (1.0 / size) + epsilon)
    scores_ref[...] = raw[0:2] * row_scale * query_scale * score_scale

    every(lambda off: exchange(*two_set, off).wait_send())


def on_device(
    hidden, out_grad, gate_weights, expert_ids, example_ids, query_ids, in_factor, out_factor
):
    n = lax.axis_size("expert")
    tokens, top, feat = hidden.shape
    exp_local = in_factor.shape[0]
    rank = out_factor.shape[1]
    model = out_grad.shape[1]
    queries = query_ids.shape[0]
    hid = jnp.transpose(hidden, (1, 0, 2)).reshape(top * tokens, feat)
    w = jnp.transpose(in_factor, (0, 2, 1)).reshape(exp_local * rank, feat)
    factor = out_factor.T
    any_spec = pl.BlockSpec(memory_space=pl.ANY)
    vmem = pl.BlockSpec(memory_space=pltpu.VMEM)
    rows_each = rank // n
    f32, bf16 = jnp.float32, jnp.bfloat16
    sketch, scores = pl.pallas_call(
        functools.partial(kernel, n),
        out_shape=(
            jax.ShapeDtypeStruct((rank // 2, EX_DEV, 2 * rank), f32),
            jax.ShapeDtypeStruct((EX_DEV, queries), f32),
        ),
        in_specs=[any_spec] * 8,
        out_specs=(vmem, vmem),
        scratch_shapes=[
            pltpu.VMEM((top, tokens), jnp.int32),
            pltpu.VMEM((top, tokens), f32),
            pltpu.VMEM((1, tokens), jnp.int32),
            pltpu.VMEM((1, queries), jnp.int32),
            pltpu.VMEM((16, tokens), f32),
            pltpu.VMEM((rank, EX_DEV * rank), f32),
            pltpu.VMEM((n, PARTS, exp_local * rank, feat // PARTS), bf16),
            pltpu.VMEM((top * tokens, feat), bf16),
            pltpu.VMEM((tokens, model), bf16),
            pltpu.VMEM((rank, model), bf16),
            pltpu.VMEM((top * tokens, 128), f32),
            pltpu.VMEM((top * tokens, 128), f32),
            pltpu.VMEM((tokens, 128), f32),
            pltpu.VMEM((tokens, 128), f32),
            pltpu.VMEM((n, rows_each, 128), f32),
            pltpu.VMEM((n, rows_each, 128), f32),
            pltpu.VMEM((n, 8, 128), f32),
            pltpu.VMEM((n, 8, 128), f32),
            pltpu.SemaphoreType.DMA((5, n // 2, PARTS)),
            pltpu.SemaphoreType.DMA((n, PARTS)),
            pltpu.SemaphoreType.DMA((10,)),
            pltpu.SemaphoreType.DMA((n,)),
            pltpu.SemaphoreType.DMA((n,)),
            pltpu.SemaphoreType.DMA((n,)),
            pltpu.SemaphoreType.DMA((n,)),
        ],
        compiler_params=pltpu.CompilerParams(
            collective_id=0, has_side_effects=True, vmem_limit_bytes=60 * 1024 * 1024
        ),
    )(
        hid, out_grad, factor, w, expert_ids.T, gate_weights.T,
        example_ids[None, :], query_ids[None, :],
    )
    sketch = jnp.transpose(sketch, (1, 0, 2))
    return (sketch.reshape(EX_DEV, rank * rank), scores)


def solution(mesh):
    in_specs = (
        P(("groups", "expert"), None, None),
        P(("groups", "expert"), None),
        P(("groups", "expert"), None),
        P(("groups", "expert"), None),
        P(("groups", "expert")),
        P("groups"),
        P("expert", None, None),
        P(),
    )
    out_specs = (P(("groups", "expert"), None), P(("groups", "expert"), None))
    return jax.shard_map(
        on_device, mesh=mesh, in_specs=in_specs, out_specs=out_specs, check_vma=False
    )
```

```python
import functools

import jax
import jax.numpy as jnp
from jax import lax
from jax.experimental import pallas as pl
from jax.experimental.pallas import tpu as pltpu
from jax.sharding import PartitionSpec as P

EX_DEV = 2
PARTS = 3

sketch_scale = 0.125
score_scale = 1.0 / 512.0
epsilon = 1e-06

MESH = pl.DeviceIdType.MESH
HIGHEST = lax.Precision.HIGHEST
NT = (((1,), (1,)), ((), ()))


def kernel(
    n, hid_hbm, og_hbm, of_hbm, w_hbm, ids_hbm, gates_hbm, example_hbm, query_hbm,
    sketch_ref, scores_ref,
    ids_in, gates_in, example_in, query_in, info_ref, sk_ref,
    wall, x_ref, og_ref, of_ref, ids_ref, gate_ref, acc_ref, gm_ref,
    part_out, part_in, gram_out, gram_in,
    send_sem, recv_sem, local_sem, s1_send, s1_recv, s2_send, s2_recv,
):
    g = lax.axis_index("groups")
    e = lax.axis_index("expert")
    zn = n // 4
    core = e % 2
    y = (e // 2) % 2
    z = e // 4
    tokens = gm_ref.shape[0]
    top = x_ref.shape[0] // tokens
    width = wall.shape[3]
    half = part_out.shape[0]

    def shard(col, zz, cc):
        return (zz * 2 + col) * 2 + cc

    barrier = pltpu.get_barrier_semaphore()
    g_other = g + 1 - 2 * (g % 2)
    pl.semaphore_signal(barrier, inc=1, device_id=(g_other, e), device_id_type=MESH)

    for there, device in (
        (z + 1 < zn, shard(y, jnp.minimum(z + 1, zn - 1), core)),
        (z >= 1, shard(y, jnp.maximum(z - 1, 0), core)),
    ):

        @pl.when(there)
        def _(device=device):
            pl.semaphore_signal(barrier, inc=1, device_id=(g, device), device_id_type=MESH)

    for device in (shard(1 - y, z, core), shard(y, z, 1 - core)):
        pl.semaphore_signal(barrier, inc=1, device_id=(g, device), device_id_type=MESH)

    own_loads = [
        pltpu.make_async_copy(
            w_hbm.at[:, p * width : (p + 1) * width], wall.at[e, p], local_sem.at[p]
        )
        for p in range(PARTS)
    ]
    og_load = pltpu.make_async_copy(og_hbm, og_ref, local_sem.at[3])
    of_load = pltpu.make_async_copy(of_hbm, of_ref, local_sem.at[4])
    x_load = pltpu.make_async_copy(hid_hbm, x_ref, local_sem.at[5])
    small_loads = [
        pltpu.make_async_copy(src, dst, local_sem.at[6 + i])
        for i, (src, dst) in enumerate(
            (
                (ids_hbm, ids_in),
                (gates_hbm, gates_in),
                (example_hbm, example_in),
                (query_hbm, query_in),
            )
        )
    ]
    for load in own_loads + small_loads + [og_load, of_load, x_load]:
        load.start()
    info_ref[...] = jnp.zeros_like(info_ref)
    acc_ref[...] = jnp.zeros_like(acc_ref)
    gram_out[...] = jnp.zeros_like(gram_out)

    pl.semaphore_wait(barrier, 3 + jnp.where(z + 1 < zn, 1, 0) + jnp.where(z >= 1, 1, 0))

    mine = 2 * (g % 2)
    theirs = 2 - mine

    up = (g, shard(y, jnp.minimum(z + 1, zn - 1), core))
    down = (g, shard(y, jnp.maximum(z - 1, 0), core))
    across = (g, shard(1 - y, z, core))
    other_x = (g_other, e)
    sibling = (g, shard(y, z, 1 - core))
    targets = (up, down, across, other_x, sibling)
    UP, DOWN, ACROSS, OTHER_X, SIBLING = range(5)

    def copy(kind, s, p):
        return pltpu.make_async_remote_copy(
            src_ref=wall.at[s, p],
            dst_ref=wall.at[s, p],
            send_sem=send_sem.at[kind, s // 2, p],
            recv_sem=recv_sem.at[s, p],
            device_id=targets[kind],
            device_id_type=MESH,
        )

    def arrived(s, p):
        copy(SIBLING, s, p).wait_recv()

    for load in own_loads:
        load.wait()

    def own_sends(act):
        for p in (mine, 1):
            act(ACROSS, e, p)
            pl.when(z + 1 < zn)(lambda p=p: act(UP, e, p))
            pl.when(z >= 1)(lambda p=p: act(DOWN, e, p))
        for p in range(PARTS):
            act(SIBLING, e, p)

    def start(kind, s, p):
        copy(kind, s, p).start()

    def finish(kind, s, p):
        copy(kind, s, p).wait_send()

    own_sends(start)

    for load in small_loads:
        load.wait()
    info_ref[0:top, :] = ids_in[...].astype(jnp.float32)
    info_ref[top : 2 * top, :] = gates_in[...]
    info_ref[2 * top : 2 * top + 1, :] = lax.rem(example_in[...], EX_DEV).astype(jnp.float32)
    table = jnp.transpose(info_ref[...])
    lane = lax.broadcasted_iota(jnp.int32, (tokens, 128), 1)
    upper = lane >= 64
    upper_f = upper.astype(jnp.float32)
    for k in range(top):
        rows = pl.ds(k * tokens, tokens)
        ids_ref[rows, :] = jnp.broadcast_to(table[:, k : k + 1], (tokens, 128)) - upper_f
        gate_ref[rows, :] = jnp.broadcast_to(table[:, top + k : top + k + 1], (tokens, 128))
    example = jnp.broadcast_to(table[:, 2 * top : 2 * top + 1], (tokens, 128))
    og_load.wait()
    of_load.wait()
    factor = of_ref[...]
    proj = lax.dot_general(
        og_ref[...], jnp.concatenate([factor, factor], axis=0), NT,
        preferred_element_type=jnp.float32,
    )
    gm_ref[...] = jnp.where(example == upper_f, proj * sketch_scale, 0.0)
    x_load.wait()

    def from_z(r, p, act):
        for kind, zs, onward in ((UP, z - r, z + 1 < zn), (DOWN, z + r, z >= 1)):

            @pl.when((zs >= 0) & (zs < zn))
            def _(kind=kind, zs=zs, onward=onward):
                s = shard(y, zs, core)
                if act is start:
                    arrived(s, p)
                pl.when(onward)(lambda: act(kind, s, p))
                act(ACROSS, s, p)
                if p is mine:
                    act(OTHER_X, s, p)
                act(SIBLING, s, p)

    def at_distance(r, body):
        def one(i, carry):
            zs = z + r * (2 * i - 1)
            pl.when((zs >= 0) & (zs < zn) & ((r > 0) | (i == 0)))(lambda: body(zs))
            return carry

        lax.fori_loop(0, 2, one, 0)

    def from_y(r, p, act):
        def body(zs):
            s = shard(1 - y, zs, core)
            if act is start:
                arrived(s, p)
            if p is mine:
                act(OTHER_X, s, p)
            act(SIBLING, s, p)

        at_distance(r, body)

    def from_x(r, col, act):
        def body(zs):
            s = shard(col, zs, core)
            if act is start:
                arrived(s, theirs)
            act(SIBLING, s, theirs)

        at_distance(r, body)

    def compute(r, col):
        def body(zs):
            place = zs * 2 + col
            for p in range(PARTS):
                arrived(place * 2 + 1 - core, p)
            weights = jnp.concatenate(
                [
                    jnp.concatenate([wall[2 * place + h, p] for p in range(PARTS)], axis=1)
                    for h in range(2)
                ],
                axis=0,
            )
            prod = lax.dot_general(
                x_ref[...], weights, NT, preferred_element_type=jnp.float32
            )
            first = (4 * place).astype(jnp.float32)
            total = acc_ref[...]
            for k in range(top):
                rows = slice(k * tokens, (k + 1) * tokens)
                ids = ids_ref[rows, :]
                chosen = jnp.where(
                    ids == first,
                    prod[rows, :128],
                    jnp.where(ids == first + 2.0, prod[rows, 128:], 0.0),
                )
                total = total + gate_ref[rows, :] * chosen
            acc_ref[...] = total

        at_distance(r, body)

    def step(t, carry):
        further = t + 1 < zn
        inside = t < zn

        @pl.when(further)
        def _():
            from_z(t + 1, mine, start)

        @pl.when(inside)
        def _():
            from_y(t, mine, start)

        @pl.when(t >= 1)
        def _():
            from_x(t - 1, 1 - y, start)

        def product(half_step, carry):
            col = jnp.where(half_step == 0, y, 1 - y)
            r = t - half_step

            @pl.when((r >= 0) & (r < zn))
            def _():
                compute(r, col)

            late = (t == zn - 1).astype(jnp.int32)

            @pl.when((half_step == 0) & further)
            def _():
                from_z(t + 1, 1, start)

            @pl.when((half_step == late) & inside)
            def _():
                from_y(t, 1, start)

            @pl.when((half_step == 0) & further)
            def _():
                from_x(t + 1, y, start)

            return carry

        lax.fori_loop(0, 2, product, 0)
        return carry

    lax.fori_loop(0, zn + 1, step, 0)

    pre = lax.dot_general(
        jnp.transpose(acc_ref[...]), gm_ref[...], (((1,), (0,)), ((), ())),
        precision=HIGHEST, preferred_element_type=jnp.float32,
    )
    sk = pre[:64] + pre[64:]
    rows_each = part_out.shape[1]
    for d in range(n):
        part_out[d] = sk[d * rows_each : (d + 1) * rows_each]

    def exchange(src, dst, send, recv, off):
        to = lax.rem(e + off, n)
        return pltpu.make_async_remote_copy(
            src_ref=src.at[to], dst_ref=dst.at[e],
            send_sem=send.at[to], recv_sem=recv.at[e],
            device_id=(g, to), device_id_type=MESH,
        )

    def incoming(src, dst, send, recv, off):
        frm = lax.rem(e + off, n)
        return pltpu.make_async_remote_copy(
            src_ref=src.at[frm], dst_ref=dst.at[frm],
            send_sem=send.at[frm], recv_sem=recv.at[frm],
            device_id=(g, frm), device_id_type=MESH,
        )

    def every(act):
        def one(off, carry):
            act(off)
            return carry

        lax.fori_loop(1, n, one, 0)

    one_set = (part_out, part_in, s1_send, s1_recv)
    two_set = (gram_out, gram_in, s2_send, s2_recv)
    every(lambda off: exchange(*one_set, off).start())
    part_in[e] = part_out[e]

    sk_ref[...] = sk
    even = sk_ref[pl.ds(0, sk.shape[0] // 2, stride=2), :]
    odd = sk_ref[pl.ds(1, sk.shape[0] // 2, stride=2), :]
    low = lax.broadcasted_iota(jnp.int32, even.shape, 1) < 64
    sketch_ref[:, 0, :] = jnp.where(low, even, pltpu.roll(odd, 64, 1))
    sketch_ref[:, 1, :] = jnp.where(low, pltpu.roll(even, 64, 1), odd)
    own_sends(finish)

    def drain(r, carry):
        for p in (mine, 1):
            pl.when(r >= 1)(lambda p=p: from_z(r, p, finish))
            from_y(r, p, finish)
        from_x(r, 1 - y, finish)
        pl.when(r >= 1)(lambda: from_x(r, y, finish))
        return carry

    lax.fori_loop(0, zn, drain, 0)
    every(lambda off: incoming(*one_set, off).wait_recv())

    slabs = [part_in[:, i, :] for i in range(rows_each)]
    zmat = jnp.concatenate(
        [
            jnp.concatenate([slab[:, :64] for slab in slabs], axis=1),
            jnp.concatenate([slab[:, 64:] for slab in slabs], axis=1),
        ],
        axis=0,
    )
    gram = lax.dot_general(
        zmat, zmat, NT, precision=HIGHEST, preferred_element_type=jnp.float32
    )
    pairs = 2 * half
    eye = lax.broadcasted_iota(jnp.int32, (pairs, pairs), 0) == lax.broadcasted_iota(
        jnp.int32, (pairs, pairs), 1
    )
    diag = jnp.sum(jnp.where(eye, gram, 0.0), axis=0, keepdims=True)
    gram_out[:, 0, :pairs] = gram[:half]
    gram_out[:, 1, :pairs] = gram[half:]
    gram_out[:, 2, :pairs] = jnp.broadcast_to(diag, (half, pairs))
    every(lambda off: exchange(*two_set, off).start())
    gram_in[e] = gram_out[e]
    every(lambda off: exchange(*one_set, off).wait_send())
    every(lambda off: incoming(*two_set, off).wait_recv())
    total = jnp.sum(gram_in[...], axis=0)

    query = query_in[...]
    column = lax.rem(query, EX_DEV) * n + lax.div(query, EX_DEV)
    count = query.shape[1]
    pick = (
        lax.broadcasted_iota(jnp.int32, (128, count), 0)
        == jnp.broadcast_to(column, (128, count))
    ).astype(jnp.float32)
    raw = jnp.dot(total, pick, precision=HIGHEST, preferred_element_type=jnp.float32)
    size = sk.shape[0] * 64
    query_scale = lax.rsqrt(raw[2:3] * (1.0 / size) + epsilon)
    place = lax.broadcasted_iota(jnp.int32, (2, 128), 0) * n + e
    own = lax.broadcasted_iota(jnp.int32, (2, 128), 1) == place
    norm = jnp.sum(jnp.where(own, total[0:2], 0.0), axis=1, keepdims=True)
    row_scale = lax.rsqrt(norm * (1.0 / size) + epsilon)
    scores_ref[...] = raw[0:2] * row_scale * query_scale * score_scale

    every(lambda off: exchange(*two_set, off).wait_send())


def on_device(
    hidden, out_grad, gate_weights, expert_ids, example_ids, query_ids, in_factor, out_factor
):
    n = lax.axis_size("expert")
    tokens, top, feat = hidden.shape
    exp_local = in_factor.shape[0]
    rank = out_factor.shape[1]
    model = out_grad.shape[1]
    queries = query_ids.shape[0]
    hid = jnp.transpose(hidden, (1, 0, 2)).reshape(top * tokens, feat)
    w = jnp.transpose(in_factor, (0, 2, 1)).reshape(exp_local * rank, feat)
    factor = out_factor.T
    any_spec = pl.BlockSpec(memory_space=pl.ANY)
    vmem = pl.BlockSpec(memory_space=pltpu.VMEM)
    rows_each = rank // n
    f32, bf16 = jnp.float32, jnp.bfloat16
    sketch, scores = pl.pallas_call(
        functools.partial(kernel, n),
        out_shape=(
            jax.ShapeDtypeStruct((rank // 2, EX_DEV, 2 * rank), f32),
            jax.ShapeDtypeStruct((EX_DEV, queries), f32),
        ),
        in_specs=[any_spec] * 8,
        out_specs=(vmem, vmem),
        scratch_shapes=[
            pltpu.VMEM((top, tokens), jnp.int32),
            pltpu.VMEM((top, tokens), f32),
            pltpu.VMEM((1, tokens), jnp.int32),
            pltpu.VMEM((1, queries), jnp.int32),
            pltpu.VMEM((16, tokens), f32),
            pltpu.VMEM((rank, EX_DEV * rank), f32),
            pltpu.VMEM((n, PARTS, exp_local * rank, feat // PARTS), bf16),
            pltpu.VMEM((top * tokens, feat), bf16),
            pltpu.VMEM((tokens, model), bf16),
            pltpu.VMEM((rank, model), bf16),
            pltpu.VMEM((top * tokens, 128), f32),
            pltpu.VMEM((top * tokens, 128), f32),
            pltpu.VMEM((tokens, 128), f32),
            pltpu.VMEM((tokens, 128), f32),
            pltpu.VMEM((n, rows_each, 128), f32),
            pltpu.VMEM((n, rows_each, 128), f32),
            pltpu.VMEM((n, 8, 128), f32),
            pltpu.VMEM((n, 8, 128), f32),
            pltpu.SemaphoreType.DMA((5, n // 2, PARTS)),
            pltpu.SemaphoreType.DMA((n, PARTS)),
            pltpu.SemaphoreType.DMA((10,)),
            pltpu.SemaphoreType.DMA((n,)),
            pltpu.SemaphoreType.DMA((n,)),
            pltpu.SemaphoreType.DMA((n,)),
            pltpu.SemaphoreType.DMA((n,)),
        ],
        compiler_params=pltpu.CompilerParams(
            collective_id=0, has_side_effects=True, vmem_limit_bytes=60 * 1024 * 1024
        ),
    )(
        hid, out_grad, factor, w, expert_ids.T, gate_weights.T,
        example_ids[None, :], query_ids[None, :],
    )
    sketch = jnp.transpose(sketch, (1, 0, 2))
    return (sketch.reshape(EX_DEV, rank * rank), scores)


def solution(mesh):
    in_specs = (
        P(("groups", "expert"), None, None),
        P(("groups", "expert"), None),
        P(("groups", "expert"), None),
        P(("groups", "expert"), None),
        P(("groups", "expert")),
        P("groups"),
        P("expert", None, None),
        P(),
    )
    out_specs = (P(("groups", "expert"), None), P(("groups", "expert"), None))
    return jax.shard_map(
        on_device, mesh=mesh, in_specs=in_specs, out_specs=out_specs, check_vma=False
    )
```
